32 devices in a mesh: grp: 4 (over z), aux: 8 (over y, x, core).
Axes of the slice: x: 2, y: 2, z: 4, core: 2. Of those that a mesh axis runs over, the one named last changes fastest.
Arguments:
- integrals: bfloat16 [1536, 512, 512], P('aux', 'grp'), may hold values from -0.01953125 to 0.01953125
- coefficients: bfloat16 [96, 8, 64], replicated, may hold values from -0.375 to 0.375
- block_lists: int32 [96, 8], replicated, may hold values from 0 to 7, as said below
- block_counts: int32 [96], replicated, may hold values from 1 to 8
Outputs:
- exchange_matrix: float32 [512, 512], P(('grp', 'aux'))
The draws below stay inside these ranges and needn't reach their ends.
Inputs may be any that keep to these rules, and one draw needn't show every extreme that they name: `block_lists`: the entries of one row are distinct blocks.
All inputs are finite; a program needn't handle non-finite values.
Results may differ from the reference program's by a relative error of at most 0.00031.
Values may be sent and summed in bfloat16 or wider, within the bound.
A program may use at most 128 MiB of HBM per device.

```python
import math
import jax
import jax.numpy as jnp
from jax import lax

BLK = 64
NBLK = 8
NW = 512
NAUX = 1536
MAXB = 8
OCC = 96


def draw_block_lists(key, part):
    keys = jax.random.split(key, OCC)
    rows = jax.vmap(lambda single: jax.random.permutation(single, NBLK)[:MAXB])(keys)
    return rows.astype(jnp.int32)


def draw_block_counts(key, part):
    base = jax.random.randint(jax.random.fold_in(key, 1), (OCC,), 1, MAXB + 1)
    place = jax.random.randint(jax.random.fold_in(key, 2), (), 0, OCC)
    return base.at[place].set(MAXB).astype(jnp.int32)


def levels(stream_key, dims, pieces, smallest, top_value):
    loudness = 1.0
    for axis_at, shards_of in pieces:
        steps = jax.random.uniform(jax.random.fold_in(jax.random.fold_in(stream_key, 6), axis_at), (shards_of,), jnp.float32, smallest / len(pieces), top_value / len(pieces))
        loudness = loudness * jnp.repeat(jnp.exp(steps), dims[axis_at] // shards_of).reshape((-1,) + (1,) * (len(dims) - 1 - axis_at))
    return loudness


def noise(stream_key, extent, width, most, cuts=(), dtype=jnp.bfloat16):
    level = levels(stream_key, extent, cuts, -0.22, 0.18) if cuts else 1.0
    entries = jax.random.normal(stream_key, extent, jnp.float32) * width * level
    return jnp.minimum(jnp.maximum(entries, -most), most).astype(dtype)


def setup_inputs(seed: int = 0) -> dict:
    seeds = jax.random.split(jax.random.key(seed), 5)
    integrals = noise(seeds[0], (NAUX, NW, NW), (NAUX * OCC * (MAXB + 1) // (2 * NBLK)) ** -0.5, 0.01953125, ((0, 8), (1, 4)))
    coefficients = noise(seeds[1], (OCC, MAXB, BLK), (BLK * (MAXB + 1) // 2) ** -0.5, 0.375)
    block_lists = draw_block_lists(jax.random.fold_in(seeds[4], 71), 0)
    block_counts = draw_block_counts(jax.random.fold_in(seeds[4], 71), 0)
    return dict(integrals=integrals, coefficients=coefficients, block_lists=block_lists, block_counts=block_counts)


def tables(block_lists, block_counts):
    slot = lax.broadcasted_iota(jnp.int32, block_lists.shape, 1)
    live_slot = slot < block_counts[:, None]
    target = lax.broadcasted_iota(jnp.int32, block_lists.shape + (NBLK,), 2)
    onehot = (block_lists[:, :, None] == target) & live_slot[:, :, None]
    return onehot.astype(jnp.float32)


def reference(integrals, coefficients, block_lists, block_counts):
    selected = tables(block_lists, block_counts)
    columns = jnp.einsum('ikb,ikj->bji', selected, coefficients.astype(jnp.float32))
    columns = columns.reshape(NW, OCC).astype(jnp.bfloat16).astype(jnp.float32)
    domain = jnp.sum(selected, axis=1)
    domain_mask = jnp.broadcast_to(domain[:, :, None], (OCC, NBLK, BLK)).reshape(OCC, NW)
    step_rows = math.gcd(NAUX, 16)
    blocks = integrals.reshape(NAUX // step_rows, step_rows, NW, NW)

    def accumulate(total, block):
        half_rows = jnp.einsum('pmn,ni->pim', block.astype(jnp.float32), columns)
        half_rows = lax.optimization_barrier(half_rows.astype(jnp.bfloat16)).astype(jnp.float32)
        masked = half_rows * domain_mask[None]
        return total + jnp.einsum('pim,pin->mn', masked, masked), None

    total, unused = lax.scan(accumulate, jnp.zeros((NW, NW), jnp.float32), blocks)
    return total
```

```python
import jax
import jax.numpy as jnp
from jax import lax
from jax.sharding import PartitionSpec as P


def block_tables(block_rows, counts, block_total):
    slot = lax.broadcasted_iota(jnp.int32, block_rows.shape, 1)
    live_slot = slot < counts[:, None]
    target = lax.broadcasted_iota(jnp.int32, block_rows.shape + (block_total,), 2)
    onehot = (block_rows[:, :, None] == target) & live_slot[:, :, None]
    return onehot.astype(jnp.bfloat16)


def shards(integrals, coefficients, block_lists, block_counts):
    window = integrals.shape[2]
    block_size = coefficients.shape[2]
    block_total = window // block_size
    orbitals = coefficients.shape[0]
    selected = block_tables(block_lists, block_counts, block_total)
    columns = jnp.einsum("ikb,ikj->bji", selected, coefficients, preferred_element_type=jnp.float32)
    columns = columns.astype(jnp.bfloat16).reshape(window, orbitals)
    half_rows = jnp.einsum(
        "pmn,ni->pim", integrals, columns, preferred_element_type=jnp.float32
    ).astype(jnp.bfloat16)
    regrouped = lax.all_to_all(half_rows, "grp", split_axis=0, concat_axis=2, tiled=True)
    domain = jnp.sum(selected, axis=1)
    domain_mask = jnp.broadcast_to(domain[:, :, None], (orbitals, block_total, block_size)).reshape(
        orbitals, window
    )
    masked = regrouped * domain_mask[None]
    partial_value = jnp.einsum("pim,pin->mn", masked, masked, preferred_element_type=jnp.float32)
    return lax.psum_scatter(partial_value, ("grp", "aux"), scatter_dimension=0, tiled=True)


def solution(mesh):
    placed = (P("aux", "grp", None), P(), P(), P())
    return jax.shard_map(
        shards, mesh=mesh, in_specs=placed, out_specs=P(("grp", "aux"), None), check_vma=False
    )
```

```python
import functools

import jax
import jax.numpy as jnp
from jax import lax
from jax.experimental import pallas as pl
from jax.experimental.pallas import tpu as pltpu
from jax.sharding import PartitionSpec as P

LANES = 128
MESH = pl.DeviceIdType.MESH
LEVELS = (64, 80)


def block_tables(block_rows, counts, block_total):
    slot = lax.broadcasted_iota(jnp.int32, block_rows.shape, 1)
    live_slot = slot < counts[:, None]
    target = lax.broadcasted_iota(jnp.int32, block_rows.shape + (block_total,), 2)
    onehot = (block_rows[:, :, None] == target) & live_slot[:, :, None]
    return onehot.astype(jnp.bfloat16)


def fused_kernel(
    groups, planes, parts, step, slots,
    integrals, packed_columns, spread, out,
    loaded, outgoing, arrived, unpacked, total, ordered,
    core_in, core_sum, plane_in, plane_sum, group_in,
    load_sem, half_send, half_recv, core_send, core_recv,
    plane_send, plane_recv, group_send, group_recv,
):
    grp, aux = lax.axis_index("grp"), lax.axis_index("aux")
    core, place = aux % 2, aux // 2
    other_core = place * 2 + (1 - core)
    orbitals = spread.shape[1] // 2
    rows_out = out.shape[0]
    depth = step * parts

    def group_at(shift):
        return (grp + shift) % groups

    def place_at(shift):
        return (place + shift) % planes

    order = [(shift + 1) % groups for shift in range(groups)]

    def load(part, shift):
        first = group_at(shift) * depth + part * step
        return pltpu.make_async_copy(
            integrals.at[pl.ds(first, step)], loaded.at[shift], load_sem.at[shift]
        )

    for shift in order:
        load(0, shift).start()

    barrier = pltpu.get_barrier_semaphore()
    partners = [(group_at(shift), aux) for shift in range(1, groups)]
    partners += [(grp, place_at(shift) * 2 + core) for shift in range(1, planes)]
    partners += [(grp, other_core)]
    for partner in partners:
        pl.semaphore_signal(barrier, inc=1, device_id=partner, device_id_type=MESH)
    pl.semaphore_wait(barrier, len(partners))

    def half_copy(part, shift, landing):
        return pltpu.make_async_remote_copy(
            src_ref=outgoing.at[shift - 1, part],
            dst_ref=arrived.at[landing, part],
            send_sem=half_send.at[shift - 1, part],
            recv_sem=half_recv.at[shift - 1, part],
            device_id=(group_at(shift), aux),
            device_id_type=MESH,
        )

    def lower_block(shape):
        return lax.broadcasted_iota(jnp.int32, shape, 1) % LANES < LANES // 2

    def transform(part, carry):
        for shift in order:
            load(part, shift).wait()
            for pair in range(step // 2):
                rows = loaded[shift, 2 * pair : 2 * pair + 2].reshape(2 * LANES, loaded.shape[3])
                both = lax.dot_general(
                    packed_columns[...], rows, (((1,), (1,)), ((), ())),
                    preferred_element_type=jnp.float32,
                )
                half = jnp.where(
                    lower_block((slots, 2 * LANES)), both[:slots], both[slots:]
                ).astype(jnp.bfloat16)
                columns = slice(pair * 2 * LANES, (pair + 1) * 2 * LANES)
                if shift:
                    outgoing[shift - 1, part, :, columns] = half
                else:
                    arrived[grp, part, :, columns] = half

            @pl.when(part + 1 < parts)
            def _():
                load(part + 1, shift).start()

            if shift:
                half_copy(part, shift, grp).start()
        return carry

    lax.fori_loop(0, parts, transform, 0)
    total[...] = jnp.zeros_like(total)

    def contract(part, carry):
        for shift in range(1, groups):
            half_copy(part, shift, group_at(groups - shift)).wait_recv()
        for source in range(groups):
            for pair in range(step // 2):
                columns = slice(pair * 2 * LANES, (pair + 1) * 2 * LANES)
                both = jnp.dot(
                    spread[source], arrived[source, part, :, columns],
                    preferred_element_type=jnp.float32,
                )
                half = jnp.where(
                    lower_block((orbitals, 2 * LANES)), both[:orbitals], both[orbitals:]
                ).astype(jnp.bfloat16)
                for side in range(2):
                    first = (2 * pair + side) * orbitals
                    unpacked[first : first + orbitals, source * LANES : (source + 1) * LANES] = (
                        half[:, side * LANES : (side + 1) * LANES]
                    )
        total[...] += lax.dot_general(
            unpacked[...], unpacked[...], (((0,), (0,)), ((), ())),
            preferred_element_type=jnp.float32,
        )
        return carry

    lax.fori_loop(0, parts, contract, 0)

    for group in range(groups):
        for spot in range(planes):
            for side in range(2):
                first = ((group * planes + spot) * 2 + side) * rows_out
                ordered[side, spot, group] = total[first : first + rows_out, :]

    def core_copy(shift):
        return pltpu.make_async_remote_copy(
            src_ref=ordered.at[1 - core, place_at(shift)],
            dst_ref=core_in.at[shift],
            send_sem=core_send.at[shift],
            recv_sem=core_recv.at[shift],
            device_id=(grp, other_core),
            device_id_type=MESH,
        )

    def plane_copy(shift):
        return pltpu.make_async_remote_copy(
            src_ref=core_sum.at[shift],
            dst_ref=plane_in.at[shift - 1],
            send_sem=plane_send.at[shift - 1],
            recv_sem=plane_recv.at[shift - 1],
            device_id=(grp, place_at(shift) * 2 + core),
            device_id_type=MESH,
        )

    def group_copy(shift):
        return pltpu.make_async_remote_copy(
            src_ref=plane_sum.at[group_at(shift)],
            dst_ref=group_in.at[shift - 1],
            send_sem=group_send.at[shift - 1],
            recv_sem=group_recv.at[shift - 1],
            device_id=(group_at(shift), aux),
            device_id_type=MESH,
        )

    places = [(shift + 1) % planes for shift in range(planes)]
    for shift in places:
        core_copy(shift).start()
    for shift in places:
        core_copy(shift).wait_recv()
        core_sum[shift] = ordered[core, place_at(shift)] + core_in[shift]
        if shift:
            plane_copy(shift).start()
    for shift in range(1, planes):
        plane_copy(shift).wait_recv()
    summed = core_sum[0]
    for shift in range(1, planes):
        summed += plane_in[shift - 1]
    plane_sum[...] = summed
    for shift in range(1, groups):
        group_copy(shift).start()
    for shift in range(1, groups):
        group_copy(shift).wait_recv()
    result = plane_sum[grp]
    for shift in range(1, groups):
        result += group_in[shift - 1]
    out[...] = result

    def drain(part, carry):
        for shift in range(1, groups):
            half_copy(part, shift, grp).wait_send()
        return carry

    lax.fori_loop(0, parts, drain, 0)
    for shift in range(planes):
        core_copy(shift).wait_send()
    for shift in range(1, planes):
        plane_copy(shift).wait_send()
    for shift in range(1, groups):
        group_copy(shift).wait_send()


def fused(slots, ident, groups, planes, parts, integrals, columns, live, rank):
    aux_rows, group_rows, window = integrals.shape
    blocks, orbitals = live.shape
    step = aux_rows // groups // parts
    rows_out = window // (groups * planes * 2)
    slot = lax.broadcasted_iota(jnp.int32, (blocks, orbitals, slots), 2)
    spread = ((rank[:, :, None] == slot) & live[:, :, None]).astype(jnp.bfloat16)
    own = lax.dynamic_slice_in_dim(spread, lax.axis_index("grp") * 2, 2, 0)
    packed_columns = jnp.einsum(
        "bis,ni->bsn", own, columns, preferred_element_type=jnp.float32
    ).astype(jnp.bfloat16).reshape(2 * slots, window)
    spread = spread.reshape(groups, 2 * orbitals, slots)
    bf16, f32, dma = jnp.bfloat16, jnp.float32, pltpu.SemaphoreType.DMA
    piece = (groups, rows_out, window)
    return pl.pallas_call(
        functools.partial(fused_kernel, groups, planes, parts, step, slots),
        out_shape=jax.ShapeDtypeStruct((rows_out, window), f32),
        in_specs=[
            pl.BlockSpec(memory_space=pl.ANY),
            pl.BlockSpec(memory_space=pltpu.VMEM),
            pl.BlockSpec(memory_space=pltpu.VMEM),
        ],
        out_specs=pl.BlockSpec(memory_space=pltpu.VMEM),
        scratch_shapes=[
            pltpu.VMEM((groups, step, group_rows, window), bf16),
            pltpu.VMEM((groups - 1, parts, slots, step * LANES), bf16),
            pltpu.VMEM((groups, parts, slots, step * LANES), bf16),
            pltpu.VMEM((step * orbitals, window), bf16),
            pltpu.VMEM((window, window), f32),
            pltpu.VMEM((2, planes) + piece, f32),
            pltpu.VMEM((planes,) + piece, f32),
            pltpu.VMEM((planes,) + piece, f32),
            pltpu.VMEM((planes - 1,) + piece, f32),
            pltpu.VMEM(piece, f32),
            pltpu.VMEM((groups - 1, rows_out, window), f32),
            dma((groups,)),
            dma((groups - 1, parts)),
            dma((groups - 1, parts)),
            dma((planes,)),
            dma((planes,)),
            dma((planes - 1,)),
            dma((planes - 1,)),
            dma((groups - 1,)),
            dma((groups - 1,)),
        ],
        compiler_params=pltpu.CompilerParams(
            collective_id=ident, has_side_effects=True, vmem_limit_bytes=48 * 1024 * 1024
        ),
    )(integrals, packed_columns, spread)


def shards(integrals, coefficients, block_lists, block_counts):
    window = integrals.shape[2]
    block_size = coefficients.shape[2]
    block_total = window // block_size
    orbitals = coefficients.shape[0]
    selected = block_tables(block_lists, block_counts, block_total)
    columns = jnp.einsum("ikb,ikj->bji", selected, coefficients, preferred_element_type=jnp.float32)
    columns = columns.astype(jnp.bfloat16).reshape(window, orbitals)
    domain = jnp.sum(selected, axis=1)
    groups, planes = lax.axis_size("grp"), lax.axis_size("aux") // 2
    per_group = integrals.shape[0] // groups
    parts = 4
    if (
        2 * block_size == LANES == integrals.shape[1]
        and per_group % (2 * parts) == 0
        and orbitals % 16 == 0
        and orbitals <= 128
    ):
        live = domain.T > 0
        rank = jnp.cumsum(live.astype(jnp.int32), axis=1) - 1
        fullest = jnp.max(rank[:, -1]) + 1
        levels = [level for level in LEVELS if level < orbitals] + [orbitals]
        branches = [
            functools.partial(fused, level, ident, groups, planes, parts)
            for ident, level in enumerate(levels)
        ]
        choice = sum((fullest > level).astype(jnp.int32) for level in levels[:-1])
        return lax.switch(choice, branches, integrals, columns, live, rank)
    half_rows = jnp.einsum(
        "pmn,ni->pim", integrals, columns, preferred_element_type=jnp.float32
    ).astype(jnp.bfloat16)
    regrouped = lax.all_to_all(half_rows, "grp", split_axis=0, concat_axis=2, tiled=True)
    domain_mask = jnp.broadcast_to(domain[:, :, None], (orbitals, block_total, block_size)).reshape(
        orbitals, window
    )
    masked = regrouped * domain_mask[None]
    partial_value = jnp.einsum("pim,pin->mn", masked, masked, preferred_element_type=jnp.float32)
    return lax.psum_scatter(partial_value, ("grp", "aux"), scatter_dimension=0, tiled=True)


def solution(mesh):
    placed = (P("aux", "grp", None), P(), P(), P())
    return jax.shard_map(
        shards, mesh=mesh, in_specs=placed, out_specs=P(("grp", "aux"), None), check_vma=False
    )
```

```python
import functools

import jax
import jax.numpy as jnp
from jax import lax
from jax.experimental import pallas as pl
from jax.experimental.pallas import tpu as pltpu
from jax.sharding import PartitionSpec as P

LANES = 128
MESH = pl.DeviceIdType.MESH
LEVELS = (24, 28, 32)


def block_tables(block_rows, counts, block_total):
    slot = lax.broadcasted_iota(jnp.int32, block_rows.shape, 1)
    live_slot = slot < counts[:, None]
    target = lax.broadcasted_iota(jnp.int32, block_rows.shape + (block_total,), 2)
    onehot = (block_rows[:, :, None] == target) & live_slot[:, :, None]
    return onehot.astype(jnp.bfloat16)


def ownership(live):
    blocks, orbitals = live.shape
    count = live.astype(jnp.int32)
    lower = lax.broadcasted_iota(jnp.int32, (blocks, 1), 0) < blocks // 2
    number = lax.broadcasted_iota(jnp.int32, (orbitals,), 0)

    def split(weight):
        pull = jnp.sum(count * weight * jnp.where(lower, 1, -1), axis=0) * orbitals + number
        place = jnp.sum((pull[None, :] > pull[:, None]).astype(jnp.int32), axis=1)
        return place, live & ((place[None, :] < orbitals // 2) != lower)

    _, first = split(jnp.full((blocks, 1), 64, jnp.int32))
    loads = jnp.sum(first.astype(jnp.int32), axis=1, keepdims=True)
    share = loads * (32 * blocks) // jnp.maximum(jnp.sum(loads), 1)
    place, cross = split(32 + share)
    return cross, jnp.where(place < orbitals // 2, place, place - orbitals // 2)


def fused_kernel(
    groups, planes, parts, step, slots, stack, owned,
    integrals, packed_columns, spread, out,
    loaded, own_out, cross_out, own_in, cross_in, stage, unpacked, total, ordered,
    core_in, core_sum, plane_in, plane_sum, group_in,
    load_sem, own_send, own_recv, cross_send, cross_recv, core_send, core_recv,
    plane_send, plane_recv, group_send, group_recv,
):
    grp, aux = lax.axis_index("grp"), lax.axis_index("aux")
    core, place = aux % 2, aux // 2
    other_core = place * 2 + (1 - core)
    side = grp % 2
    base = grp - side
    facing = (base + 2) % groups
    partner_group = base + 1 - side
    padded = (slots + 7) // 8 * 8
    rows_out = out.shape[0]

    def group_at(shift):
        return (grp + shift) % groups

    def place_at(shift):
        return (place + shift) % planes

    def rows_half(turn):
        return 1 - side if turn == 0 else side

    def load(part, turn):
        first = (rows_half(turn) * parts + part) * step
        return pltpu.make_async_copy(
            integrals.at[pl.ds(first, step)], loaded.at[turn], load_sem.at[turn]
        )

    for turn in range(2):
        load(0, turn).start()

    barrier = pltpu.get_barrier_semaphore()
    partners = [(group_at(shift), aux) for shift in range(1, groups)]
    partners += [(grp, place_at(shift) * 2 + core) for shift in range(1, planes)]
    partners += [(grp, other_core)]
    for partner in partners:
        pl.semaphore_signal(barrier, inc=1, device_id=partner, device_id_type=MESH)
    pl.semaphore_wait(barrier, len(partners))

    def own_copy(part, landing):
        return pltpu.make_async_remote_copy(
            src_ref=own_out.at[part],
            dst_ref=own_in.at[landing, part],
            send_sem=own_send.at[part],
            recv_sem=own_recv.at[part],
            device_id=(partner_group, aux),
            device_id_type=MESH,
        )

    def cross_copy(part, turn, landing):
        return pltpu.make_async_remote_copy(
            src_ref=cross_out.at[turn, part],
            dst_ref=cross_in.at[landing, part],
            send_sem=cross_send.at[turn, part],
            recv_sem=cross_recv.at[turn, part],
            device_id=(facing + rows_half(turn), aux),
            device_id_type=MESH,
        )

    def joined(lower, upper):
        lane = lax.broadcasted_iota(jnp.int32, lower.shape, 1) % LANES
        return jnp.where(lane < LANES // 2, lower, upper)

    tile = 2 * LANES
    tiles = step // 2 // stack

    def transform(part, carry):
        for turn in range(2):
            load(part, turn).wait()
            for pair in range(step // 2):
                rows = loaded[turn, 2 * pair : 2 * pair + 2].reshape(tile, loaded.shape[3])
                both = lax.dot_general(
                    packed_columns[...], rows, (((1,), (1,)), ((), ())),
                    preferred_element_type=jnp.float32,
                )
                mine = joined(both[:owned], both[owned : 2 * owned]).astype(jnp.bfloat16)
                columns = slice(pair * tile, (pair + 1) * tile)
                if turn == 0:
                    own_out[part, :, columns] = mine
                else:
                    own_in[side, part, :, columns] = mine
                theirs = joined(
                    both[2 * owned : 2 * owned + padded],
                    both[2 * owned + padded : 2 * owned + 2 * padded],
                )
                level, column = pair % stack, pair // stack
                stage[level * slots : level * slots + padded, :] = theirs
                if level == stack - 1:
                    cross_out[turn, part, :, column * tile : (column + 1) * tile] = stage[
                        : stack * slots, :
                    ].astype(jnp.bfloat16)

            @pl.when(part + 1 < parts)
            def _():
                load(part + 1, turn).start()

            cross_copy(part, turn, side).start()
            if turn == 0:
                own_copy(part, side).start()
        return carry

    lax.fori_loop(0, parts, transform, 0)
    total[...] = jnp.zeros_like(total)

    def contract(part, carry):
        own_copy(part, 1 - side).wait_recv()
        for turn in range(2):
            cross_copy(part, turn, rows_half(turn)).wait_recv()
        for pair in range(step // 2):
            level, column = pair % stack, pair // stack
            for source in range(4):
                if source < 2:
                    half = own_in[source, part, :, pair * tile : (pair + 1) * tile]
                else:
                    both = jnp.dot(
                        spread[source - 2, level],
                        cross_in[source - 2, part, :, column * tile : (column + 1) * tile],
                        preferred_element_type=jnp.float32,
                    )
                    half = joined(both[:owned], both[owned:]).astype(jnp.bfloat16)
                for half_tile in range(2):
                    first = (2 * pair + half_tile) * owned
                    unpacked[first : first + owned, source * LANES : (source + 1) * LANES] = (
                        half[:, half_tile * LANES : (half_tile + 1) * LANES]
                    )
        total[...] += lax.dot_general(
            unpacked[...], unpacked[...], (((0,), (0,)), ((), ())),
            preferred_element_type=jnp.float32,
        )
        return carry

    lax.fori_loop(0, parts, contract, 0)

    middle = total.shape[1] // 2
    for group in range(groups):
        for spot in range(planes):
            for half_core in range(2):
                first = ((group * planes + spot) * 2 + half_core) * rows_out
                rows = total[first : first + rows_out, :]
                turned = jnp.concatenate([rows[:, middle:], rows[:, :middle]], axis=1)
                ordered[half_core, spot, (base + group) % groups] = jnp.where(
                    base == 0, rows, turned
                )

    def core_copy(shift):
        return pltpu.make_async_remote_copy(
            src_ref=ordered.at[1 - core, place_at(shift)],
            dst_ref=core_in.at[shift],
            send_sem=core_send.at[shift],
            recv_sem=core_recv.at[shift],
            device_id=(grp, other_core),
            device_id_type=MESH,
        )

    def plane_copy(shift):
        return pltpu.make_async_remote_copy(
            src_ref=core_sum.at[shift],
            dst_ref=plane_in.at[shift - 1],
            send_sem=plane_send.at[shift - 1],
            recv_sem=plane_recv.at[shift - 1],
            device_id=(grp, place_at(shift) * 2 + core),
            device_id_type=MESH,
        )

    def group_copy(shift):
        return pltpu.make_async_remote_copy(
            src_ref=plane_sum.at[group_at(shift)],
            dst_ref=group_in.at[shift - 1],
            send_sem=group_send.at[shift - 1],
            recv_sem=group_recv.at[shift - 1],
            device_id=(group_at(shift), aux),
            device_id_type=MESH,
        )

    places = [(shift + 1) % planes for shift in range(planes)]
    for shift in places:
        core_copy(shift).start()
    for shift in places:
        core_copy(shift).wait_recv()
        core_sum[shift] = ordered[core, place_at(shift)] + core_in[shift]
        if shift:
            plane_copy(shift).start()
    for shift in range(1, planes):
        plane_copy(shift).wait_recv()
    summed = core_sum[0]
    for shift in range(1, planes):
        summed += plane_in[shift - 1]
    plane_sum[...] = summed
    for shift in range(1, groups):
        group_copy(shift).start()
    for shift in range(1, groups):
        group_copy(shift).wait_recv()
    result = plane_sum[grp]
    for shift in range(1, groups):
        result += group_in[shift - 1]
    out[...] = result

    def drain(part, carry):
        own_copy(part, side).wait_send()
        for turn in range(2):
            cross_copy(part, turn, side).wait_send()
        return carry

    lax.fori_loop(0, parts, drain, 0)
    for shift in range(planes):
        core_copy(shift).wait_send()
    for shift in range(1, planes):
        plane_copy(shift).wait_send()
    for shift in range(1, groups):
        group_copy(shift).wait_send()


def fused(slots, ident, groups, planes, parts, integrals, columns, live, cross, rank, seat):
    aux_rows, group_rows, window = integrals.shape
    blocks, orbitals = live.shape
    owned = orbitals // 2
    step = aux_rows // 2 // parts
    stack = 1
    while stack * slots % 16:
        stack *= 2
    padded = (slots + 7) // 8 * 8
    rows_out = window // (groups * planes * 2)
    bf = jnp.bfloat16
    chair = lax.broadcasted_iota(jnp.int32, (orbitals, owned), 1)
    seated = (seat[:, None] == chair).astype(bf)
    slot = lax.broadcasted_iota(jnp.int32, (blocks, orbitals, padded), 2)
    sent = ((rank[:, :, None] == slot) & cross[:, :, None]).astype(bf)
    kept = seated[None] * (live & ~cross)[:, :, None].astype(bf)
    grp = lax.axis_index("grp")
    mine = lax.dynamic_slice_in_dim(jnp.concatenate([kept, sent], axis=2), grp * 2, 2, 0)
    packed_columns = jnp.einsum(
        "bis,ni->bsn", mine, columns, preferred_element_type=jnp.float32
    ).astype(bf)
    packed_columns = jnp.concatenate(
        [packed_columns[:, :owned].reshape(2 * owned, window),
         packed_columns[:, owned:].reshape(2 * padded, window)], axis=0
    )
    facing = lax.dynamic_slice_in_dim(sent, (groups // 2 - grp // 2 * 2) * 2, blocks // 2, 0)
    spread = jnp.einsum("it,bis->bts", seated, facing, preferred_element_type=jnp.float32)
    spread = spread.astype(bf)[:, :, :slots].reshape(2, 2 * owned, slots)
    spread = jnp.stack(
        [jnp.pad(spread, ((0, 0), (0, 0), (level * slots, (stack - 1 - level) * slots)))
         for level in range(stack)], axis=1
    )
    lanes = step * LANES
    bf16, f32, dma = jnp.bfloat16, jnp.float32, pltpu.SemaphoreType.DMA
    piece = (groups, rows_out, window)
    return pl.pallas_call(
        functools.partial(
            fused_kernel, groups, planes, parts, step, slots, stack, owned
        ),
        out_shape=jax.ShapeDtypeStruct((rows_out, window), f32),
        in_specs=[
            pl.BlockSpec(memory_space=pl.ANY),
            pl.BlockSpec(memory_space=pltpu.VMEM),
            pl.BlockSpec(memory_space=pltpu.VMEM),
        ],
        out_specs=pl.BlockSpec(memory_space=pltpu.VMEM),
        scratch_shapes=[
            pltpu.VMEM((2, step, group_rows, window), bf16),
            pltpu.VMEM((parts, owned, lanes), bf16),
            pltpu.VMEM((2, parts, stack * slots, lanes // stack), bf16),
            pltpu.VMEM((2, parts, owned, lanes), bf16),
            pltpu.VMEM((2, parts, stack * slots, lanes // stack), bf16),
            pltpu.VMEM((stack * slots + 8, 2 * LANES), f32),
            pltpu.VMEM((step * owned, window), bf16),
            pltpu.VMEM((window, window), f32),
            pltpu.VMEM((2, planes) + piece, f32),
            pltpu.VMEM((planes,) + piece, f32),
            pltpu.VMEM((planes,) + piece, f32),
            pltpu.VMEM((planes - 1,) + piece, f32),
            pltpu.VMEM(piece, f32),
            pltpu.VMEM((groups - 1, rows_out, window), f32),
            dma((2,)),
            dma((parts,)),
            dma((parts,)),
            dma((2, parts)),
            dma((2, parts)),
            dma((planes,)),
            dma((planes,)),
            dma((planes - 1,)),
            dma((planes - 1,)),
            dma((groups - 1,)),
            dma((groups - 1,)),
        ],
        compiler_params=pltpu.CompilerParams(
            collective_id=ident, has_side_effects=True, vmem_limit_bytes=48 * 1024 * 1024
        ),
    )(integrals, packed_columns, spread)


def shards(integrals, coefficients, block_lists, block_counts):
    window = integrals.shape[2]
    block_size = coefficients.shape[2]
    block_total = window // block_size
    orbitals = coefficients.shape[0]
    selected = block_tables(block_lists, block_counts, block_total)
    columns = jnp.einsum("ikb,ikj->bji", selected, coefficients, preferred_element_type=jnp.float32)
    columns = columns.astype(jnp.bfloat16).reshape(window, orbitals)
    domain = jnp.sum(selected, axis=1)
    groups, planes = lax.axis_size("grp"), lax.axis_size("aux") // 2
    parts = 12
    if (
        groups == 4
        and 2 * block_size == LANES == integrals.shape[1]
        and integrals.shape[0] % (16 * parts) == 0
        and orbitals % 32 == 0
        and orbitals <= 128
    ):
        live = domain.T > 0
        cross, seat = ownership(live)
        rank = jnp.cumsum(cross.astype(jnp.int32), axis=1) - 1
        fullest = jnp.max(rank[:, -1]) + 1
        levels = [level for level in LEVELS if level < orbitals // 2] + [orbitals // 2]
        branches = [
            functools.partial(fused, level, ident, groups, planes, parts)
            for ident, level in enumerate(levels)
        ]
        choice = sum((fullest > level).astype(jnp.int32) for level in levels[:-1])
        return lax.switch(choice, branches, integrals, columns, live, cross, rank, seat)
    half_rows = jnp.einsum(
        "pmn,ni->pim", integrals, columns, preferred_element_type=jnp.float32
    ).astype(jnp.bfloat16)
    regrouped = lax.all_to_all(half_rows, "grp", split_axis=0, concat_axis=2, tiled=True)
    domain_mask = jnp.broadcast_to(domain[:, :, None], (orbitals, block_total, block_size)).reshape(
        orbitals, window
    )
    masked = regrouped * domain_mask[None]
    partial_value = jnp.einsum("pim,pin->mn", masked, masked, preferred_element_type=jnp.float32)
    return lax.psum_scatter(partial_value, ("grp", "aux"), scatter_dimension=0, tiled=True)


def solution(mesh):
    placed = (P("aux", "grp", None), P(), P(), P())
    return jax.shard_map(
        shards, mesh=mesh, in_specs=placed, out_specs=P(("grp", "aux"), None), check_vma=False
    )
```

```python
import functools

import jax
import jax.numpy as jnp
from jax import lax
from jax.experimental import pallas as pl
from jax.experimental.pallas import tpu as pltpu
from jax.sharding import PartitionSpec as P

LANES = 128
MESH = pl.DeviceIdType.MESH
LEVELS = (24, 28, 32)


def block_tables(block_rows, counts, block_total):
    slot = lax.broadcasted_iota(jnp.int32, block_rows.shape, 1)
    live_slot = slot < counts[:, None]
    target = lax.broadcasted_iota(jnp.int32, block_rows.shape + (block_total,), 2)
    onehot = (block_rows[:, :, None] == target) & live_slot[:, :, None]
    return onehot.astype(jnp.bfloat16)


def ownership(live):
    blocks, orbitals = live.shape
    count = live.astype(jnp.int32)
    lower = lax.broadcasted_iota(jnp.int32, (blocks, 1), 0) < blocks // 2
    number = lax.broadcasted_iota(jnp.int32, (orbitals,), 0)

    def split(weight):
        pull = jnp.sum(count * weight * jnp.where(lower, 1, -1), axis=0) * orbitals + number
        place = jnp.sum((pull[None, :] > pull[:, None]).astype(jnp.int32), axis=1)
        return place, live & ((place[None, :] < orbitals // 2) != lower)

    weight = jnp.full((blocks, 1), 64, jnp.int32)
    usual = orbitals * 11 // 48
    for gain in (4, 3, 2, 1):
        _, cross = split(weight)
        loads = jnp.sum(cross.astype(jnp.int32), axis=1, keepdims=True)
        weight = weight + (loads - usual) * gain // 2
    place, cross = split(weight)
    return cross, jnp.where(place < orbitals // 2, place, place - orbitals // 2)


def fused_kernel(
    groups, planes, parts, step, slots, stack, owned,
    integrals, packed_columns, spread, out,
    loaded, own_out, cross_out, own_in, cross_in, stage, unpacked, total, ordered,
    core_in, core_sum, plane_in, plane_sum, group_in,
    load_sem, own_send, own_recv, cross_send, cross_recv, core_send, core_recv,
    plane_send, plane_recv, group_send, group_recv,
):
    grp, aux = lax.axis_index("grp"), lax.axis_index("aux")
    core, place = aux % 2, aux // 2
    other_core = place * 2 + (1 - core)
    side = grp % 2
    base = grp - side
    facing = (base + 2) % groups
    partner_group = base + 1 - side
    padded = (slots + 7) // 8 * 8
    rows_out = out.shape[0]

    def group_at(shift):
        return (grp + shift) % groups

    def place_at(shift):
        return (place + shift) % planes

    def rows_half(turn):
        return 1 - side if turn == 0 else side

    def load(part, turn):
        first = (rows_half(turn) * parts + part) * step
        return pltpu.make_async_copy(
            integrals.at[pl.ds(first, step)], loaded.at[turn], load_sem.at[turn]
        )

    for turn in range(2):
        load(0, turn).start()

    barrier = pltpu.get_barrier_semaphore()
    partners = [(group_at(shift), aux) for shift in range(1, groups)]
    partners += [(grp, place_at(shift) * 2 + core) for shift in range(1, planes)]
    partners += [(grp, other_core)]
    for partner in partners:
        pl.semaphore_signal(barrier, inc=1, device_id=partner, device_id_type=MESH)
    pl.semaphore_wait(barrier, len(partners))

    def own_copy(part, landing):
        return pltpu.make_async_remote_copy(
            src_ref=own_out.at[part],
            dst_ref=own_in.at[landing, part],
            send_sem=own_send.at[part],
            recv_sem=own_recv.at[part],
            device_id=(partner_group, aux),
            device_id_type=MESH,
        )

    def cross_copy(part, turn, landing):
        return pltpu.make_async_remote_copy(
            src_ref=cross_out.at[turn, part],
            dst_ref=cross_in.at[landing, part],
            send_sem=cross_send.at[turn, part],
            recv_sem=cross_recv.at[turn, part],
            device_id=(facing + rows_half(turn), aux),
            device_id_type=MESH,
        )

    def joined(lower, upper):
        lane = lax.broadcasted_iota(jnp.int32, lower.shape, 1) % LANES
        return jnp.where(lane < LANES // 2, lower, upper)

    tile = 2 * LANES
    tiles = step // 2 // stack

    def transform(part, carry):
        for turn in range(2):
            load(part, turn).wait()
            for pair in range(step // 2):
                rows = loaded[turn, 2 * pair : 2 * pair + 2].reshape(tile, loaded.shape[3])
                both = lax.dot_general(
                    packed_columns[...], rows, (((1,), (1,)), ((), ())),
                    preferred_element_type=jnp.float32,
                )
                mine = joined(both[:owned], both[owned : 2 * owned]).astype(jnp.bfloat16)
                columns = slice(pair * tile, (pair + 1) * tile)
                if turn == 0:
                    own_out[part, :, columns] = mine
                else:
                    own_in[side, part, :, columns] = mine
                theirs = joined(
                    both[2 * owned : 2 * owned + padded],
                    both[2 * owned + padded : 2 * owned + 2 * padded],
                )
                level, column = pair % stack, pair // stack
                stage[level * slots : level * slots + padded, :] = theirs
                if level == stack - 1:
                    cross_out[turn, part, :, column * tile : (column + 1) * tile] = stage[
                        : stack * slots, :
                    ].astype(jnp.bfloat16)

            @pl.when(part + 1 < parts)
            def _():
                load(part + 1, turn).start()

            cross_copy(part, turn, side).start()
            if turn == 0:
                own_copy(part, side).start()
        return carry

    lax.fori_loop(0, parts, transform, 0)
    total[...] = jnp.zeros_like(total)

    def contract(part, carry):
        own_copy(part, 1 - side).wait_recv()
        for turn in range(2):
            cross_copy(part, turn, rows_half(turn)).wait_recv()
        for pair in range(step // 2):
            level, column = pair % stack, pair // stack
            for source in range(4):
                if source < 2:
                    half = own_in[source, part, :, pair * tile : (pair + 1) * tile]
                else:
                    both = jnp.dot(
                        spread[source - 2, level],
                        cross_in[source - 2, part, :, column * tile : (column + 1) * tile],
                        preferred_element_type=jnp.float32,
                    )
                    half = joined(both[:owned], both[owned:]).astype(jnp.bfloat16)
                for half_tile in range(2):
                    first = (2 * pair + half_tile) * owned
                    unpacked[first : first + owned, source * LANES : (source + 1) * LANES] = (
                        half[:, half_tile * LANES : (half_tile + 1) * LANES]
                    )
        total[...] += lax.dot_general(
            unpacked[...], unpacked[...], (((0,), (0,)), ((), ())),
            preferred_element_type=jnp.float32,
        )
        return carry

    lax.fori_loop(0, parts, contract, 0)

    middle = total.shape[1] // 2
    for group in range(groups):
        for spot in range(planes):
            for half_core in range(2):
                first = ((group * planes + spot) * 2 + half_core) * rows_out
                rows = total[first : first + rows_out, :]
                turned = jnp.concatenate([rows[:, middle:], rows[:, :middle]], axis=1)
                ordered[half_core, spot, (base + group) % groups] = jnp.where(
                    base == 0, rows, turned
                )

    def core_copy(shift):
        return pltpu.make_async_remote_copy(
            src_ref=ordered.at[1 - core, place_at(shift)],
            dst_ref=core_in.at[shift],
            send_sem=core_send.at[shift],
            recv_sem=core_recv.at[shift],
            device_id=(grp, other_core),
            device_id_type=MESH,
        )

    def plane_copy(shift):
        return pltpu.make_async_remote_copy(
            src_ref=core_sum.at[shift],
            dst_ref=plane_in.at[shift - 1],
            send_sem=plane_send.at[shift - 1],
            recv_sem=plane_recv.at[shift - 1],
            device_id=(grp, place_at(shift) * 2 + core),
            device_id_type=MESH,
        )

    def group_copy(shift):
        return pltpu.make_async_remote_copy(
            src_ref=plane_sum.at[group_at(shift)],
            dst_ref=group_in.at[shift - 1],
            send_sem=group_send.at[shift - 1],
            recv_sem=group_recv.at[shift - 1],
            device_id=(group_at(shift), aux),
            device_id_type=MESH,
        )

    places = [(shift + 1) % planes for shift in range(planes)]
    for shift in places:
        core_copy(shift).start()
    for shift in places:
        core_copy(shift).wait_recv()
        core_sum[shift] = ordered[core, place_at(shift)] + core_in[shift]
        if shift:
            plane_copy(shift).start()
    for shift in range(1, planes):
        plane_copy(shift).wait_recv()
    summed = core_sum[0]
    for shift in range(1, planes):
        summed += plane_in[shift - 1]
    plane_sum[...] = summed
    for shift in range(1, groups):
        group_copy(shift).start()
    for shift in range(1, groups):
        group_copy(shift).wait_recv()
    result = plane_sum[grp]
    for shift in range(1, groups):
        result += group_in[shift - 1]
    out[...] = result

    def drain(part, carry):
        own_copy(part, side).wait_send()
        for turn in range(2):
            cross_copy(part, turn, side).wait_send()
        return carry

    lax.fori_loop(0, parts, drain, 0)
    for shift in range(planes):
        core_copy(shift).wait_send()
    for shift in range(1, planes):
        plane_copy(shift).wait_send()
    for shift in range(1, groups):
        group_copy(shift).wait_send()


def fused(slots, ident, groups, planes, parts, integrals, columns, live, cross, rank, seat):
    aux_rows, group_rows, window = integrals.shape
    blocks, orbitals = live.shape
    owned = orbitals // 2
    step = aux_rows // 2 // parts
    stack = 1
    while stack * slots % 16:
        stack *= 2
    padded = (slots + 7) // 8 * 8
    rows_out = window // (groups * planes * 2)
    bf = jnp.bfloat16
    chair = lax.broadcasted_iota(jnp.int32, (orbitals, owned), 1)
    seated = (seat[:, None] == chair).astype(bf)
    slot = lax.broadcasted_iota(jnp.int32, (blocks, orbitals, padded), 2)
    sent = ((rank[:, :, None] == slot) & cross[:, :, None]).astype(bf)
    kept = seated[None] * (live & ~cross)[:, :, None].astype(bf)
    grp = lax.axis_index("grp")
    mine = lax.dynamic_slice_in_dim(jnp.concatenate([kept, sent], axis=2), grp * 2, 2, 0)
    packed_columns = jnp.einsum(
        "bis,ni->bsn", mine, columns, preferred_element_type=jnp.float32
    ).astype(bf)
    packed_columns = jnp.concatenate(
        [packed_columns[:, :owned].reshape(2 * owned, window),
         packed_columns[:, owned:].reshape(2 * padded, window)], axis=0
    )
    facing = lax.dynamic_slice_in_dim(sent, (groups // 2 - grp // 2 * 2) * 2, blocks // 2, 0)
    spread = jnp.einsum("it,bis->bts", seated, facing, preferred_element_type=jnp.float32)
    spread = spread.astype(bf)[:, :, :slots].reshape(2, 2 * owned, slots)
    spread = jnp.stack(
        [jnp.pad(spread, ((0, 0), (0, 0), (level * slots, (stack - 1 - level) * slots)))
         for level in range(stack)], axis=1
    )
    lanes = step * LANES
    bf16, f32, dma = jnp.bfloat16, jnp.float32, pltpu.SemaphoreType.DMA
    piece = (groups, rows_out, window)
    return pl.pallas_call(
        functools.partial(
            fused_kernel, groups, planes, parts, step, slots, stack, owned
        ),
        out_shape=jax.ShapeDtypeStruct((rows_out, window), f32),
        in_specs=[
            pl.BlockSpec(memory_space=pl.ANY),
            pl.BlockSpec(memory_space=pltpu.VMEM),
            pl.BlockSpec(memory_space=pltpu.VMEM),
        ],
        out_specs=pl.BlockSpec(memory_space=pltpu.VMEM),
        scratch_shapes=[
            pltpu.VMEM((2, step, group_rows, window), bf16),
            pltpu.VMEM((parts, owned, lanes), bf16),
            pltpu.VMEM((2, parts, stack * slots, lanes // stack), bf16),
            pltpu.VMEM((2, parts, owned, lanes), bf16),
            pltpu.VMEM((2, parts, stack * slots, lanes // stack), bf16),
            pltpu.VMEM((stack * slots + 8, 2 * LANES), f32),
            pltpu.VMEM((step * owned, window), bf16),
            pltpu.VMEM((window, window), f32),
            pltpu.VMEM((2, planes) + piece, f32),
            pltpu.VMEM((planes,) + piece, f32),
            pltpu.VMEM((planes,) + piece, f32),
            pltpu.VMEM((planes - 1,) + piece, f32),
            pltpu.VMEM(piece, f32),
            pltpu.VMEM((groups - 1, rows_out, window), f32),
            dma((2,)),
            dma((parts,)),
            dma((parts,)),
            dma((2, parts)),
            dma((2, parts)),
            dma((planes,)),
            dma((planes,)),
            dma((planes - 1,)),
            dma((planes - 1,)),
            dma((groups - 1,)),
            dma((groups - 1,)),
        ],
        compiler_params=pltpu.CompilerParams(
            collective_id=ident, has_side_effects=True, vmem_limit_bytes=48 * 1024 * 1024
        ),
    )(integrals, packed_columns, spread)


def shards(integrals, coefficients, block_lists, block_counts):
    window = integrals.shape[2]
    block_size = coefficients.shape[2]
    block_total = window // block_size
    orbitals = coefficients.shape[0]
    selected = block_tables(block_lists, block_counts, block_total)
    columns = jnp.einsum("ikb,ikj->bji", selected, coefficients, preferred_element_type=jnp.float32)
    columns = columns.astype(jnp.bfloat16).reshape(window, orbitals)
    domain = jnp.sum(selected, axis=1)
    groups, planes = lax.axis_size("grp"), lax.axis_size("aux") // 2
    parts = 12
    if (
        groups == 4
        and 2 * block_size == LANES == integrals.shape[1]
        and integrals.shape[0] % (16 * parts) == 0
        and orbitals % 32 == 0
        and orbitals <= 128
    ):
        live = domain.T > 0
        cross, seat = ownership(live)
        rank = jnp.cumsum(cross.astype(jnp.int32), axis=1) - 1
        fullest = jnp.max(rank[:, -1]) + 1
        levels = [level for level in LEVELS if level < orbitals // 2] + [orbitals // 2]
        branches = [
            functools.partial(fused, level, ident, groups, planes, parts)
            for ident, level in enumerate(levels)
        ]
        choice = sum((fullest > level).astype(jnp.int32) for level in levels[:-1])
        return lax.switch(choice, branches, integrals, columns, live, cross, rank, seat)
    half_rows = jnp.einsum(
        "pmn,ni->pim", integrals, columns, preferred_element_type=jnp.float32
    ).astype(jnp.bfloat16)
    regrouped = lax.all_to_all(half_rows, "grp", split_axis=0, concat_axis=2, tiled=True)
    domain_mask = jnp.broadcast_to(domain[:, :, None], (orbitals, block_total, block_size)).reshape(
        orbitals, window
    )
    masked = regrouped * domain_mask[None]
    partial_value = jnp.einsum("pim,pin->mn", masked, masked, preferred_element_type=jnp.float32)
    return lax.psum_scatter(partial_value, ("grp", "aux"), scatter_dimension=0, tiled=True)


def solution(mesh):
    placed = (P("aux", "grp", None), P(), P(), P())
    return jax.shard_map(
        shards, mesh=mesh, in_specs=placed, out_specs=P(("grp", "aux"), None), check_vma=False
    )
```
